128 devices in a mesh: row: 8 (over x, core), ch: 16 (over y, z).
Axes of the slice: x: 4, y: 4, z: 4, core: 2. Of those that a mesh axis runs over, the one named last changes fastest.
Arguments:
- surface_rows: float32 [4, 8, 896, 1024], P(None, None, 'ch', 'row'), may hold values from -6 to 6
- he_states: float32 [256, 1024], P(None, 'row'), may hold values from -0.1875 to 0.1875
- energies: float32 [256], replicated, may hold values from -2 to 2
- state_phase: float32 [256], replicated, may hold values from -3.140625 to 3.140625
- momentum_phase: float32 [256], replicated, may hold values from -3.140625 to 3.140625
- bessel_value: float32 [32, 256], replicated, may hold values from -6 to 6
- bessel_slope: float32 [32, 256], replicated, may hold values from -6 to 6
- channel_l2: int32 [896], replicated, may hold values from 0 to 31
- surface_list: int32 [896], P('ch'), may hold values from 0 to 895, each once
- previous: float32 [896, 256, 2, 256], P(None, ('row', 'ch')), may hold values from -6 to 6
- coupling: float32 [2048, 896], replicated, may hold values from -0.1875 to 0.1875
Outputs:
- amplitudes: float32 [896, 256, 2, 256], P(None, ('row', 'ch'))
- spectrum: float32 [2048, 256, 2, 256], P(None, ('row', 'ch'))
The draws below stay inside these ranges and needn't reach their ends.
Inputs may be any that keep to these rules, and one draw needn't show every extreme that they name: `surface_list`: each channel number appears exactly once.
All inputs are finite; a program needn't handle non-finite values.
Results may differ from the reference program's by a relative error of at most 0.0001.
Values sent between devices are 32-bit elements; how exact they have to be, the bound alone decides.
A program may use at most 128 MiB of HBM per device.

```python
import jax
import jax.numpy as jnp
from jax import lax

NCH = 896
NR = 1024
STEPS = 8
NB = 256
NK = 256
LMAX = 32
NG = 2048


def plant(array, own_key, smallest, top_value):
    longest = array.shape.index(max(array.shape))
    spots = []
    for shift in (0, 1):
        where = [jax.random.randint(jax.random.fold_in(own_key, axis), (), 0, length) for axis, length in enumerate(array.shape)]
        where[longest] = (where[longest] + shift) % array.shape[longest]
        spots.append(tuple(where))
    return array.at[spots[0]].set(smallest).at[spots[1]].set(top_value)


def steps_of(key, extent, pieces, least, high):
    level = 1.0
    for axis_at, blocks in pieces:
        steps = jax.random.uniform(jax.random.fold_in(jax.random.fold_in(key, 6), axis_at), (blocks,), jnp.float32, least / len(pieces), high / len(pieces))
        level = level * jnp.repeat(jnp.exp(steps), extent[axis_at] // blocks).reshape((-1,) + (1,) * (len(extent) - 1 - axis_at))
    return level


def bell_draw(own_key, dims, scale, reach, split=(), kind=jnp.bfloat16):
    values = scale * jax.random.normal(own_key, dims, jnp.float32)
    if split:
        values = values * steps_of(own_key, dims, split, -0.22, 0.18)
    return jnp.clip(values, -reach, reach).astype(kind)


def setup_inputs(seed: int = 0) -> dict:
    arg_keys = jax.random.split(jax.random.key(seed), 12)
    surface_rows = bell_draw(arg_keys[0], (4, STEPS, NCH, NR), 1.0, 6.0, ((2, 16), (3, 8)), jnp.float32)
    he_states = bell_draw(arg_keys[1], (NB, NR), NR ** -0.5, 0.1875, ((1, 8),), jnp.float32)
    energies = jnp.clip(jax.random.uniform(arg_keys[2], (NB,), jnp.float32, -2.0, 2.0), -2.0, 2.0)
    state_phase = jnp.clip(jax.random.uniform(arg_keys[3], (NB,), jnp.float32, -3.140625, 3.140625), -3.140625, 3.140625)
    momentum_phase = jnp.clip(jax.random.uniform(arg_keys[4], (NK,), jnp.float32, -3.140625, 3.140625), -3.140625, 3.140625)
    bessel_value = bell_draw(arg_keys[5], (LMAX, NK), 1.0, 6.0, (), jnp.float32)
    bessel_slope = bell_draw(arg_keys[6], (LMAX, NK), 1.0, 6.0, (), jnp.float32)
    channel_l2 = plant(jax.random.randint(arg_keys[7], (NCH,), 0, LMAX), jax.random.fold_in(arg_keys[7], 1), 0, LMAX - 1).astype(jnp.int32)
    surface_list = jax.random.permutation(arg_keys[8], NCH).astype(jnp.int32)
    previous = bell_draw(arg_keys[9], (NCH, NB, 2, NK), 1.0, 6.0, ((1, 128),), jnp.float32)
    coupling = bell_draw(arg_keys[10], (NG, NCH), NCH ** -0.5, 0.1875, (), jnp.float32)
    return {"surface_rows": surface_rows, "he_states": he_states, "energies": energies, "state_phase": state_phase, "momentum_phase": momentum_phase, "bessel_value": bessel_value, "bessel_slope": bessel_slope, "channel_l2": channel_l2, "surface_list": surface_list, "previous": previous, "coupling": coupling}


highest = lax.Precision.HIGHEST
time_step = 0.4
momentum_top = 2.0


def lookup(levels, table_rows):
    one_hot = (levels[:, None] == jnp.arange(table_rows.shape[0], dtype=jnp.int32)[None, :]).astype(table_rows.dtype)
    return jnp.dot(one_hot, table_rows, precision=highest, preferred_element_type=jnp.float32)


def volkov(projected, bessel_at, slope_at, state_energy, state_angle, momentum_angle):
    window = projected.shape[2]
    momenta_count = bessel_at.shape[1]
    times = jnp.arange(window, dtype=jnp.float32) * time_step
    momenta = (jnp.arange(momenta_count, dtype=jnp.float32) + 0.5) * (momentum_top / momenta_count)
    angles = state_energy[:, None] * times[None, :]
    cos_state = jnp.cos(angles)[:, :, None]
    sin_state = jnp.sin(angles)[:, :, None]
    value_re = projected[:, 0] * cos_state - projected[:, 1] * sin_state
    value_im = projected[:, 0] * sin_state + projected[:, 1] * cos_state
    slope_re = projected[:, 2] * cos_state - projected[:, 3] * sin_state
    slope_im = projected[:, 2] * sin_state + projected[:, 3] * cos_state
    momentum_angles = 0.5 * times[:, None] * (momenta * momenta)[None, :]
    cos_momentum = jnp.cos(momentum_angles)
    sin_momentum = jnp.sin(momentum_angles)

    def time_sum(part_re, part_im):
        summed_re = jnp.einsum("ntc,tk->nck", part_re, cos_momentum, precision=highest) - jnp.einsum("ntc,tk->nck", part_im, sin_momentum, precision=highest)
        summed_im = jnp.einsum("ntc,tk->nck", part_re, sin_momentum, precision=highest) + jnp.einsum("ntc,tk->nck", part_im, cos_momentum, precision=highest)
        return summed_re, summed_im

    surf_re, surf_im = time_sum(value_re, value_im)
    deriv_re, deriv_im = time_sum(slope_re, slope_im)
    flux_re = bessel_at[None] * deriv_re - slope_at[None] * surf_re
    flux_im = bessel_at[None] * deriv_im - slope_at[None] * surf_im
    global_angle = state_angle[:, None] + momentum_angle[None, :]
    cos_global = jnp.cos(global_angle)[:, None, :]
    sin_global = jnp.sin(global_angle)[:, None, :]
    result_re = 0.5 * time_step * (flux_re * cos_global - flux_im * sin_global)
    result_im = 0.5 * time_step * (flux_re * sin_global + flux_im * cos_global)
    return jnp.stack([result_re, result_im], axis=2)


def reference(surface_rows, he_states, energies, state_phase, momentum_phase, bessel_value, bessel_slope, channel_l2, surface_list, previous, coupling):
    projected = jnp.einsum("qtcr,nr->nqtc", surface_rows, he_states, precision=highest)
    levels = channel_l2[surface_list]
    bessel_at = lookup(levels, bessel_value)
    slope_at = lookup(levels, bessel_slope)
    block_size = min(32, NB)
    blocks = []
    for number in range(NB // block_size):
        begin_row = number * block_size
        blocks.append(volkov(projected[begin_row:begin_row + block_size], bessel_at, slope_at,
                             energies[begin_row:begin_row + block_size], state_phase[begin_row:begin_row + block_size], momentum_phase))
    fresh_part = jnp.transpose(jnp.concatenate(blocks, axis=0), (1, 0, 2, 3))
    placed = jnp.zeros_like(fresh_part).at[surface_list].set(fresh_part)
    amplitudes = previous + placed
    spectrum = jnp.dot(coupling, amplitudes.reshape(NCH, -1), precision=highest, preferred_element_type=jnp.float32).reshape(NG, NB, 2, NK)
    return amplitudes, spectrum
```

```python
import functools
import jax, jax.numpy as jnp
from jax import lax
from jax.experimental import pallas as pl
from jax.experimental.pallas import tpu as pltpu
from jax.sharding import PartitionSpec as P

f32, bf16, i32 = jnp.float32, jnp.bfloat16, jnp.int32
time_step, momentum_top = 0.4, 2.0
NCH, NG = 896, 2048
ANY = pl.BlockSpec(memory_space=pl.ANY)
VM = pl.BlockSpec(memory_space=pltpu.VMEM)
SM = pl.BlockSpec(memory_space=pltpu.SMEM)

def split2(x):
    hi = x.astype(bf16).astype(f32)
    return hi, x - hi

def dot(a, b):
    return lax.dot_general(a, b, (((1,), (0,)), ((), ())), preferred_element_type=f32)

MESH = pl.DeviceIdType.MESH
NT = (((1,), (1,)), ((), ()))
HALF = 896


def exchange_kernel(surf_hbm, he_ref, own_list, z_ref, l_ref,
                    own_s, other, own, got, rel, fromx, ybuf,
                    load_sem, core_send, core_recv, rel_send, rel_recv,
                    dir_send, dir_recv, comb_send, comb_recv,
                    out_send, out_recv, list_send, list_recv):
    row, ch = lax.axis_index("row"), lax.axis_index("ch")
    x, core = row // 2, row % 2
    right, left, across = (x + 1) % 4, (x + 3) % 4, (x + 2) % 4
    partner = {"row": 2 * x + 1 - core}
    to_right, to_left = {"row": 2 * right + core}, {"row": 2 * left + core}

    load = pltpu.make_async_copy(surf_hbm, own_s, load_sem)
    load.start()
    barrier = pltpu.get_barrier_semaphore()
    for target in (partner, to_right, to_left):
        pl.semaphore_signal(barrier, inc=1, device_id=target, device_id_type=MESH)
    for d in range(1, 16):
        pl.semaphore_signal(barrier, inc=1, device_id={"ch": (ch + d) % 16}, device_id_type=MESH)

    parts = []
    for side in (1 - core, core):
        for n in range(2):
            for xx in range(4):
                parts.append(he_ref[xx, side, pl.ds(n, 16, stride=2), :])
    he = jnp.concatenate(parts, axis=0)
    h_hi, h_lo = split2(he)
    h_left = jnp.concatenate([h_hi, h_hi, h_lo], axis=1).astype(bf16)
    for n in range(2):
        for tail in (14, 15):
            ybuf[n, pl.ds(tail, 16, stride=16), :] = jnp.zeros((16, 128), f32)
    load.wait()
    for jc in range(7):
        rows = jnp.concatenate([own_s[pl.ds(jc * 8 + j, 32, stride=56), :] for j in range(8)], axis=0)
        s_hi, s_lo = split2(rows)
        s_right = jnp.concatenate([s_hi, s_lo, s_hi], axis=1).astype(bf16)
        part = lax.dot_general(h_left, s_right, NT, preferred_element_type=f32)
        lanes = slice(jc * 256, (jc + 1) * 256)
        for n in range(2):
            for xx in range(4):
                at = (n * 4 + xx) * 16
                other[n, xx, :, lanes] = part[at:at + 16]
                own[n, xx, :, lanes] = part[128 + at:144 + at]
    pl.semaphore_wait(barrier, 18)

    def remote(src, dst, send, recv, target):
        return pltpu.make_async_remote_copy(src_ref=src, dst_ref=dst, send_sem=send, recv_sem=recv,
                                            device_id=target, device_id_type=MESH)

    core_copies = [remote(other.at[n], got.at[n], core_send.at[n], core_recv.at[n], partner) for n in range(2)]
    for copy in core_copies:
        copy.start()
    here = pl.ds(pl.multiple_of(ch * 16, 16), 16)
    list_copies = [remote(own_list, l_ref.at[here], list_send.at[d], list_recv.at[d], {"ch": (ch + d) % 16})
                   for d in range(1, 16)]
    for copy in list_copies:
        copy.start()
    l_ref[here] = own_list[...]

    halves = (pl.ds(0, HALF), pl.ds(HALF, HALF))
    relays, directs, combs, outs = [], [], [], []
    for n in range(2):
        core_copies[n].wait()
        for h, target in ((0, to_right), (1, to_left)):
            own[n, across, :, halves[h]] += got[n, across, :, halves[h]]
            relays.append(remote(own.at[n, across, :, halves[h]], rel.at[n, h], rel_send.at[n, h],
                                 rel_recv.at[n, h], target))
            relays[-1].start()
        for h, target, block in ((1, to_right, right), (0, to_left, left)):
            own[n, block, :, halves[h]] += got[n, block, :, halves[h]]
            directs.append(remote(own.at[n, block, :, halves[h]], fromx.at[n, 1 - h, :, halves[h]],
                                  dir_send.at[n, h], dir_recv.at[n, h], target))
            directs[-1].start()
        for h, block in ((0, right), (1, left)):
            own[n, block, :, halves[h]] += got[n, block, :, halves[h]]
        own[n, x] += got[n, x]
    for n in range(2):
        for h, target, block in ((0, to_right, right), (1, to_left, left)):
            relays[2 * n + h].wait()
            own[n, block, :, halves[h]] += rel[n, h]
            combs.append(remote(own.at[n, block, :, halves[h]], fromx.at[n, h, :, halves[h]],
                                comb_send.at[n, h], comb_recv.at[n, h], target))
            combs[-1].start()
    for n in range(2):
        for copy in directs[2 * n:2 * n + 2] + combs[2 * n:2 * n + 2]:
            copy.wait()
        for jhi in range(14):
            lanes = slice(jhi * 128, (jhi + 1) * 128)
            ybuf[n, pl.ds(jhi, 16, stride=16), :] = own[n, x, :, lanes] + (fromx[n, 0, :, lanes] + fromx[n, 1, :, lanes])
        for d in range(1, 16):
            peer = (ch + d) % 16
            outs.append(remote(ybuf.at[n, pl.ds(pl.multiple_of(peer * 16, 16), 16)], z_ref.at[n, here],
                               out_send.at[n, d], out_recv.at[n, d], {"ch": peer}))
            outs[-1].start()
        z_ref[n, here] = ybuf[n, here]
    for copy in list_copies + outs:
        copy.wait()


def exchange(surf, he, own_list):
    dma = pltpu.SemaphoreType.DMA
    return pl.pallas_call(
        exchange_kernel,
        out_shape=(jax.ShapeDtypeStruct((2, 256, 128), f32), jax.ShapeDtypeStruct((256, 128), i32)),
        in_specs=[ANY, VM, VM],
        out_specs=(VM, VM),
        scratch_shapes=[pltpu.VMEM((1792, 128), f32), pltpu.VMEM((2, 4, 16, 1792), f32), pltpu.VMEM((2, 4, 16, 1792), f32),
                        pltpu.VMEM((2, 4, 16, 1792), f32), pltpu.VMEM((2, 2, 16, HALF), f32),
                        pltpu.VMEM((2, 2, 16, 1792), f32), pltpu.VMEM((2, 256, 128), f32),
                        dma, dma((2,)), dma((2,)), dma((2, 2)), dma((2, 2)), dma((2, 2)), dma((2, 2)),
                        dma((2, 2)), dma((2, 2)), dma((2, 16)), dma((2, 16)), dma((16,)), dma((16,))],
        compiler_params=pltpu.CompilerParams(vmem_limit_bytes=40 * 2**20, collective_id=0, has_side_effects=True),
        name="exchange",
    )(surf, he, own_list)


def spread_kernel(rows, es_ref, z_ref, l_ref, lev_ref, bv_ref, bs_ref, mp_ref, prev_hbm, coup_ref,
                  amp_hbm, spec_ref,
                  prev, ampo, ahi, alo, psem, asem):
    step = pl.program_id(0)
    steps = pl.num_programs(0)
    chunk = 128
    nchunk = NCH // chunk

    def prev_copy(i):
        return pltpu.make_async_copy(prev_hbm.at[pl.ds(i * chunk, chunk)], prev.at[pl.ds(i * chunk, chunk)], psem.at[i])

    def amp_copy(i):
        return pltpu.make_async_copy(ampo.at[pl.ds(i * chunk, chunk)], amp_hbm.at[pl.ds(i * chunk, chunk)], asem.at[i])

    @pl.when(step == 0)
    def _():
        for i in range(nchunk):
            prev_copy(i).start()
        z = [z_ref[0], z_ref[1]]
        pieces = []
        for a in z:
            hi, lo = split2(a)
            pieces.append((hi, lo))
        order = [pieces[0][0], pieces[1][0], pieces[0][1], pieces[1][1]]
        rights = []
        for jlo in range(4):
            parts = [a[:, jlo * 32:(jlo + 1) * 32] for a in order]
            one = jnp.concatenate(parts, axis=1)
            rights.append(jnp.concatenate([one, one], axis=1).astype(bf16))
        lt = jnp.transpose(l_ref[...])
        lev = lev_ref[...]
        io = lax.broadcasted_iota(i32, (128, NCH), 0)
        sel = ((io % 32 == jnp.broadcast_to(lev, (128, NCH))) & (io < 96)).astype(f32)
        selt = jnp.transpose(sel).astype(bf16)
        def three(t):
            a, r = split2(t)
            b, r = split2(r)
            return jnp.concatenate([a, b, r, jnp.zeros_like(a)], axis=0).astype(bf16)
        table = jnp.concatenate([three(bv_ref[...]), three(bs_ref[...])], axis=1)
        momenta = (lax.broadcasted_iota(i32, (8, 256), 1).astype(f32) + 0.5) * (momentum_top / 256)
        times = lax.broadcasted_iota(i32, (8, 256), 0).astype(f32) * time_step
        zeros = jnp.zeros((8, 128), f32)
        facts = []
        for n in range(2):
            ang = es_ref[0, n] * times + 0.5 * times * (momenta * momenta) + (es_ref[1, n] + mp_ref[...])
            co = (0.5 * time_step) * jnp.cos(ang)
            si = (0.5 * time_step) * jnp.sin(ang)
            for khi in range(2):
                c, s = co[:, khi * 128:(khi + 1) * 128], si[:, khi * 128:(khi + 1) * 128]
                blk = jnp.concatenate([jnp.concatenate([c, s], 1), jnp.concatenate([-s, c], 1)], 0)
                hi, lo = split2(blk)
                z16 = jnp.zeros((16, 256), f32)
                for d in range(2):
                    def piece(b):
                        own = [z16, z16]
                        own[d] = b
                        two = [z16, z16] * 2
                        two[2 * n], two[2 * n + 1] = own
                        return two
                    rowsl = piece(hi) + piece(hi) + piece(lo) + piece(lo)
                    facts.append(jnp.concatenate(rowsl, axis=0).astype(bf16))
        for i in range(nchunk):
            rs = pl.ds(i * chunk, chunk)
            ioc = lax.broadcasted_iota(i32, (chunk, 256), 0) + i * chunk
            r = None
            for jlo in range(4):
                one = (ioc == jnp.broadcast_to(lt[jlo * 32:jlo * 32 + 1, :], (chunk, 256))).astype(f32).astype(bf16)
                t = dot(one, rights[jlo])
                r = t if r is None else r + t
            left = r.astype(bf16)
            bt = dot(selt[i * chunk:(i + 1) * chunk], table)
            prev_copy(i).wait()
            for n in range(2):
                for khi in range(2):
                    su = dot(left, facts[(n * 2 + khi) * 2])
                    de = dot(left, facts[(n * 2 + khi) * 2 + 1])
                    bvc = bt[:, khi * 128:(khi + 1) * 128]
                    bsc = bt[:, 256 + khi * 128:256 + (khi + 1) * 128]
                    for p in range(2):
                        sidx = n * 4 + khi * 2 + p
                        fr = bvc * de[:, p * 128:(p + 1) * 128] - bsc * su[:, p * 128:(p + 1) * 128]
                        am = prev[rs, sidx, :] + fr
                        ampo[rs, sidx, :] = am
                        h = am.astype(bf16)
                        ahi[rs, sidx * 128:(sidx + 1) * 128] = h
                        alo[rs, sidx * 128:(sidx + 1) * 128] = (am - h.astype(f32)).astype(bf16)
            amp_copy(i).start()

    c = coup_ref[...]
    chi = c.astype(bf16)
    clo = (c - chi.astype(f32)).astype(bf16)
    for s in range(4):
        cs = slice(s * 256, (s + 1) * 256)
        both = dot(jnp.concatenate([chi, clo], 0), ahi[:, cs])
        res = both[:rows] + both[rows:] + dot(chi, alo[:, cs])
        spec_ref[:, 2 * s, :] = res[:, :128]
        spec_ref[:, 2 * s + 1, :] = res[:, 128:]

    @pl.when(step == steps - 1)
    def _():
        for i in range(nchunk):
            amp_copy(i).wait()

def spread(es, z, lists, lev, bv, bs, mp, prev, coup, rows=256):
    return pl.pallas_call(
        functools.partial(spread_kernel, rows),
        grid=(NG // rows,),
        out_shape=(jax.ShapeDtypeStruct((NCH, 8, 128), f32), jax.ShapeDtypeStruct((NG, 8, 128), f32)),
        in_specs=[SM, VM, VM, VM, VM, VM, VM, ANY, pl.BlockSpec((rows, NCH), lambda i: (i, 0))],
        out_specs=(ANY, pl.BlockSpec((rows, 8, 128), lambda i: (i, 0, 0))),
        scratch_shapes=[pltpu.VMEM((NCH, 8, 128), f32), pltpu.VMEM((NCH, 8, 128), f32),
                        pltpu.VMEM((NCH, 1024), bf16), pltpu.VMEM((NCH, 1024), bf16),
                        pltpu.SemaphoreType.DMA((7,)), pltpu.SemaphoreType.DMA((7,))],
        compiler_params=pltpu.CompilerParams(vmem_limit_bytes=56 * 2**20),
        cost_estimate=pl.CostEstimate(flops=3*2*2048*896*1024, bytes_accessed=24*2**20, transcendentals=0),
        name="spread",
    )(es, z, lists, lev, bv, bs, mp, prev, coup)


def shards(surface_rows, he_states, energies, state_phase, momentum_phase, bessel_value, bessel_slope,
           channel_l2, surface_list, previous, coupling):
    surf = surface_rows.reshape(1792, 128)
    he = he_states.reshape(4, 2, 32, 128)
    own_list = jnp.repeat(jnp.pad(surface_list.reshape(14, 4), ((0, 2), (0, 0)), constant_values=-1), 32, axis=1)
    projected, listed = exchange(surf, he, own_list)
    first = (lax.axis_index("row") * 16 + lax.axis_index("ch")) * 2
    states = jnp.stack([lax.dynamic_slice_in_dim(energies, first, 2, 0), lax.dynamic_slice_in_dim(state_phase, first, 2, 0)])
    prev = previous.reshape(NCH, 2, 2, 2, 128).transpose(0, 1, 3, 2, 4).reshape(NCH, 8, 128)
    amplitudes, spectrum = spread(states, projected, listed, channel_l2.reshape(1, NCH), bessel_value, bessel_slope,
                                  momentum_phase.reshape(1, 256), prev, coupling)

    def whole(a):
        return a.reshape(-1, 2, 2, 2, 128).transpose(0, 1, 3, 2, 4).reshape(-1, 2, 2, 256)

    return whole(amplitudes), whole(spectrum)


def solution(mesh):
    split = P(None, ("row", "ch"), None, None)
    return jax.shard_map(
        shards,
        mesh=mesh,
        in_specs=(P(None, None, "ch", "row"), P(None, "row"), P(), P(), P(), P(), P(), P(), P("ch"), split, P()),
        out_specs=(split, split),
        check_vma=False,
    )
```

```python
import jax
import jax.numpy as jnp
from jax import lax
from jax.experimental import pallas as pl
from jax.experimental.pallas import tpu as pltpu
from jax.sharding import PartitionSpec as P

f32, bf16, i32 = jnp.float32, jnp.bfloat16, jnp.int32
time_step, momentum_top = 0.4, 2.0
NCH, NG = 896, 2048
HALF = 896
PART = 256
ANY = pl.BlockSpec(memory_space=pl.ANY)
VM = pl.BlockSpec(memory_space=pltpu.VMEM)
HBM = pl.BlockSpec(memory_space=pltpu.HBM)
MESH = pl.DeviceIdType.MESH
NT = (((1,), (1,)), ((), ()))


def split2(x):
    hi = x.astype(bf16).astype(f32)
    return hi, x - hi


def dot(a, b):
    return lax.dot_general(a, b, (((1,), (0,)), ((), ())), preferred_element_type=f32)


def exchange_kernel(surf_hbm, he_hbm, list_hbm, energy_hbm, phase_hbm, mp_hbm, bv_hbm, bs_hbm, lev_hbm, prev_hbm,
                    coup_hbm, z_ref, hot_ref, bt_ref, fact_ref, left_ref, prev_ref,
                    own_s, he_v, list_ref, energy_ref, phase_ref, mp_v, bv_v, bs_v, lev_v, stage, other, own, got, rel, fromx, ybuf, own_list, lists,
                    load_sem, prev_sem, coup_sem, core_send, core_recv, rel_send, rel_recv,
                    dir_send, dir_recv, comb_send, comb_recv, out_send, out_recv, list_send, list_recv):
    row, ch = lax.axis_index("row"), lax.axis_index("ch")
    x, core = row // 2, row % 2
    right, left, across = (x + 1) % 4, (x + 3) % 4, (x + 2) % 4
    partner = {"row": 2 * x + 1 - core}
    to_right, to_left = {"row": 2 * right + core}, {"row": 2 * left + core}

    loads = [pltpu.make_async_copy(src, dst, load_sem.at[k]) for k, (src, dst) in enumerate((
        (he_hbm, he_v), (surf_hbm, own_s), (list_hbm, list_ref), (energy_hbm, energy_ref), (phase_hbm, phase_ref),
        (mp_hbm, mp_v), (bv_hbm, bv_v), (bs_hbm, bs_v), (lev_hbm, lev_v)))]
    for load in loads:
        load.start()
    barrier = pltpu.get_barrier_semaphore()
    for target in (partner, to_right, to_left):
        pl.semaphore_signal(barrier, inc=1, device_id=target, device_id_type=MESH)
    for d in range(1, 16):
        pl.semaphore_signal(barrier, inc=1, device_id={"ch": (ch + d) % 16}, device_id_type=MESH)

    def coup_copy(k):
        return pltpu.make_async_copy(coup_hbm.at[pl.ds(k * PART, PART)], stage.at[k % 2], coup_sem.at[k % 2])

    prev_copies = [pltpu.make_async_copy(prev_hbm.at[:, s, :], prev_ref.at[:, pl.ds(s * 128, 128)], prev_sem.at[s])
                   for s in range(8)]

    loads[0].wait()
    parts = []
    for side in (1 - core, core):
        for n in range(2):
            for xx in range(4):
                parts.append(he_v[xx, side, pl.ds(n, 16, stride=2), :])
    he = jnp.concatenate(parts, axis=0)
    h_hi, h_lo = split2(he)
    h_left = jnp.concatenate([h_hi, h_hi, h_lo], axis=1).astype(bf16)
    loads[1].wait()
    for k in range(2):
        coup_copy(k).start()
    for copy in prev_copies:
        copy.start()
    for jc in range(7):
        rows = jnp.concatenate([own_s[pl.ds(jc * 8 + j, 32, stride=56), :] for j in range(8)], axis=0)
        s_hi, s_lo = split2(rows)
        s_right = jnp.concatenate([s_hi, s_lo, s_hi], axis=1).astype(bf16)
        part = lax.dot_general(h_left, s_right, NT, preferred_element_type=f32)
        lanes = slice(jc * 256, (jc + 1) * 256)
        for n in range(2):
            for xx in range(4):
                at = (n * 4 + xx) * 16
                other[n, xx, :, lanes] = part[at:at + 16]
                own[n, xx, :, lanes] = part[128 + at:144 + at]

    place = lax.broadcasted_iota(i32, (16, 128), 0) * 4 + lax.broadcasted_iota(i32, (16, 128), 1) // 32
    listed = jnp.full((16, 128), -1, i32)
    loads[2].wait()
    for j in range(56):
        listed = jnp.where(place == j, list_ref[j], listed)
    own_list[...] = listed
    pl.semaphore_wait(barrier, 18)

    def remote(src, dst, send, recv, target):
        return pltpu.make_async_remote_copy(src_ref=src, dst_ref=dst, send_sem=send, recv_sem=recv,
                                            device_id=target, device_id_type=MESH)

    def core_copy(n, k):
        block = (across, right, left, x)[k]
        return remote(other.at[n, block], got.at[n, block], core_send.at[n, k], core_recv.at[n, k], partner)

    for n, k in ((0, 0), (0, 1), (0, 2), (1, 0), (1, 1), (1, 2), (0, 3), (1, 3)):
        core_copy(n, k).start()
    here = pl.ds(pl.multiple_of(ch * 16, 16), 16)
    list_copies = [remote(own_list, lists.at[here], list_send.at[d], list_recv.at[d], {"ch": (ch + d) % 16})
                   for d in range(1, 16)]

    halves = (pl.ds(0, HALF), pl.ds(HALF, HALF))
    relays, directs, combs, outs = [], [], [], []

    def add_core(n, k):
        block = (across, right, left, x)[k]
        core_copy(n, k).wait()
        own[n, block] += got[n, block]

    for n in range(2):
        add_core(n, 0)
        for h, target in ((0, to_right), (1, to_left)):
            relays.append(remote(own.at[n, across, :, halves[h]], rel.at[n, h], rel_send.at[n, h],
                                 rel_recv.at[n, h], target))
            relays[-1].start()
        for k, h, target, block in ((1, 1, to_right, right), (2, 0, to_left, left)):
            add_core(n, k)
            directs.append(remote(own.at[n, block, :, halves[h]], fromx.at[n, 1 - h, :, halves[h]],
                                  dir_send.at[n, h], dir_recv.at[n, h], target))
            directs[-1].start()
    for copy in list_copies:
        copy.start()
    lists[here] = listed
    for n in range(2):
        add_core(n, 3)

    for load in loads[3:]:
        load.wait()
    momenta = (lax.broadcasted_iota(i32, (8, 256), 1).astype(f32) + 0.5) * (momentum_top / 256)
    times = lax.broadcasted_iota(i32, (8, 256), 0).astype(f32) * time_step
    z16 = jnp.zeros((16, 256), f32)
    first = (row * 16 + ch) * 2
    for n in range(2):
        angle = energy_ref[first + n] * times + 0.5 * times * (momenta * momenta) + (phase_ref[first + n] + mp_v[...])
        cos, sin = (0.5 * time_step) * jnp.cos(angle), (0.5 * time_step) * jnp.sin(angle)
        for khi in range(2):
            c, s = cos[:, khi * 128:(khi + 1) * 128], sin[:, khi * 128:(khi + 1) * 128]
            block = jnp.concatenate([jnp.concatenate([c, s], 1), jnp.concatenate([-s, c], 1)], 0)
            for d in range(2):
                spread_rows = []
                for piece in split2(block):
                    four = [z16] * 4
                    four[2 * n + d] = piece
                    spread_rows += four * 2
                fact_ref[(n * 2 + khi) * 2 + d] = jnp.concatenate(spread_rows, axis=0).astype(bf16)

    def three(table):
        a, rest = split2(table)
        b, rest = split2(rest)
        return jnp.concatenate([a, b, rest, jnp.zeros_like(a)], axis=0).astype(bf16)

    table = jnp.concatenate([three(bv_v[...]), three(bs_v[...])], axis=1)
    level_of = lax.broadcasted_iota(i32, (128, 128), 0)
    for i in range(7):
        chosen = (level_of % 32 == jnp.broadcast_to(lev_v[i:i + 1, :], (128, 128))) & (level_of < 96)
        bt_ref[i * 128:(i + 1) * 128, :] = dot(jnp.transpose(chosen.astype(f32)).astype(bf16), table)

    def split_coupling(k):
        coup_copy(k).wait()

        def some(i, _):
            at = pl.multiple_of(i * 32, 32)
            c = stage[k % 2, pl.ds(at, 32), :]
            hi = c.astype(bf16)
            to = pl.ds(pl.multiple_of(k * PART + i * 32, 32), 32)
            left_ref[to, 0:NCH] = hi
            left_ref[to, NCH:2 * NCH] = (c - hi.astype(f32)).astype(bf16)
            left_ref[to, 2 * NCH:3 * NCH] = hi
            return 0

        lax.fori_loop(0, PART // 32, some, 0)
        if k + 2 < NG // PART:
            coup_copy(k + 2).start()

    split_coupling(0)
    split_coupling(1)
    for n in range(2):
        for h, target, block in ((0, to_right, right), (1, to_left, left)):
            relays[2 * n + h].wait()
            own[n, block, :, halves[h]] += rel[n, h]
            combs.append(remote(own.at[n, block, :, halves[h]], fromx.at[n, h, :, halves[h]],
                                comb_send.at[n, h], comb_recv.at[n, h], target))
            combs[-1].start()
        split_coupling(2 + n)

    for copy in list_copies:
        copy.wait()
    row_of = jnp.transpose(lists[...])
    for i in range(7):
        channel = lax.broadcasted_iota(i32, (128, 256), 0) + i * 128
        for jlo in range(4):
            match = channel == jnp.broadcast_to(row_of[jlo * 32:jlo * 32 + 1, :], (128, 256))
            hot_ref[i * 128:(i + 1) * 128, jlo * 256:(jlo + 1) * 256] = match.astype(f32).astype(bf16)
    for n in range(2):
        for tail in (14, 15):
            ybuf[n, pl.ds(tail, 16, stride=16), :] = jnp.zeros((16, 128), f32)
    for n in range(2):
        for copy in directs[2 * n:2 * n + 2] + combs[2 * n:2 * n + 2]:
            copy.wait()
        for jhi in range(14):
            lanes = slice(jhi * 128, (jhi + 1) * 128)
            ybuf[n, pl.ds(jhi, 16, stride=16), :] = own[n, x, :, lanes] + (fromx[n, 0, :, lanes] + fromx[n, 1, :, lanes])
        for d in range(1, 16):
            peer = (ch + d) % 16
            outs.append(remote(ybuf.at[n, pl.ds(pl.multiple_of(peer * 16, 16), 16)], z_ref.at[n, here],
                               out_send.at[n, d], out_recv.at[n, d], {"ch": peer}))
            outs[-1].start()
        z_ref[n, here] = ybuf[n, here]
        split_coupling(4 + 2 * n)
        split_coupling(5 + 2 * n)
    for copy in prev_copies:
        copy.wait()
    for copy in outs:
        copy.wait()


def exchange(*operands):
    dma = pltpu.SemaphoreType.DMA
    block = pltpu.VMEM((2, 4, 16, 1792), f32)
    return pl.pallas_call(
        exchange_kernel,
        out_shape=(jax.ShapeDtypeStruct((2, 256, 128), f32), jax.ShapeDtypeStruct((NCH, 1024), bf16),
                   jax.ShapeDtypeStruct((NCH, 512), f32), jax.ShapeDtypeStruct((8, 256, 256), bf16),
                   jax.ShapeDtypeStruct((NG, 3 * NCH), bf16), jax.ShapeDtypeStruct((NCH, 1024), f32)),
        in_specs=[HBM] * 11,
        out_specs=(VM,) * 6,
        scratch_shapes=[pltpu.VMEM((1792, 128), f32), pltpu.VMEM((4, 2, 32, 128), f32), pltpu.SMEM((56,), i32),
                        pltpu.SMEM((256,), f32), pltpu.SMEM((256,), f32), pltpu.VMEM((1, 256), f32),
                        pltpu.VMEM((32, 256), f32), pltpu.VMEM((32, 256), f32), pltpu.VMEM((7, 128), i32),
                        pltpu.VMEM((2, PART, NCH), f32), block, block, block,
                        pltpu.VMEM((2, 2, 16, HALF), f32), pltpu.VMEM((2, 2, 16, 1792), f32), pltpu.VMEM((2, 256, 128), f32),
                        pltpu.VMEM((16, 128), i32), pltpu.VMEM((256, 128), i32),
                        dma((9,)), dma((8,)), dma((2,)), dma((2, 4)), dma((2, 4)), dma((2, 2)), dma((2, 2)),
                        dma((2, 2)), dma((2, 2)), dma((2, 2)), dma((2, 2)), dma((2, 16)), dma((2, 16)), dma((16,)), dma((16,))],
        compiler_params=pltpu.CompilerParams(vmem_limit_bytes=20 * 2**20, collective_id=0, has_side_effects=True),
        cost_estimate=pl.CostEstimate(flops=10**8, bytes_accessed=14 * 2**20, transcendentals=0),
        name="exchange",
    )(*(pltpu.with_memory_space_constraint(a, pltpu.HBM) for a in operands))


def spread_kernel(z_ref, hot_ref, bt_ref, fact_ref, left_ref, prev_ref, amp_hbm, spec_hbm,
                  right, ampo, obuf, asem, osem):
    chunk, mrows, slots = 128, 512, 4
    nchunk = NCH // chunk
    (hi0, lo0), (hi1, lo1) = split2(z_ref[0]), split2(z_ref[1])
    picks = []
    for jlo in range(4):
        one = jnp.concatenate([a[:, jlo * 32:(jlo + 1) * 32] for a in (hi0, hi1, lo0, lo1)], axis=1)
        picks.append(jnp.concatenate([one, one], axis=1).astype(bf16))
    picks = jnp.concatenate(picks, axis=0)

    def amp_copy(s):
        return pltpu.make_async_copy(ampo.at[:, pl.ds(s * 128, 128)], amp_hbm.at[:, s, :], asem.at[s])

    for i in range(nchunk):
        at = pl.ds(i * chunk, chunk)
        chosen = dot(hot_ref[at, :], picks).astype(bf16)
        for n in range(2):
            for khi in range(2):
                surf = dot(chosen, fact_ref[(n * 2 + khi) * 2])
                slope = dot(chosen, fact_ref[(n * 2 + khi) * 2 + 1])
                value_at = bt_ref[at, khi * 128:(khi + 1) * 128]
                slope_at = bt_ref[at, 256 + khi * 128:256 + (khi + 1) * 128]
                for p in range(2):
                    s = n * 4 + khi * 2 + p
                    lanes = slice(p * 128, (p + 1) * 128)
                    cols = slice(s * 128, (s + 1) * 128)
                    total = prev_ref[at, cols] + (value_at * slope[:, lanes] - slope_at * surf[:, lanes])
                    ampo[at, cols] = total
                    hi = total.astype(bf16)
                    right[at, cols] = hi
                    right[pl.ds(NCH + i * chunk, chunk), cols] = hi
                    right[pl.ds(2 * NCH + i * chunk, chunk), cols] = (total - hi.astype(f32)).astype(bf16)
    for s in range(8):
        amp_copy(s).start()

    def out_copy(u, s):
        n, m = todo[u]
        return pltpu.make_async_copy(obuf.at[u % slots, :, pl.ds(s * 128, 128)],
                                     spec_hbm.at[pl.ds(m * mrows, mrows), 4 * n + s, :], osem.at[u % slots, s])

    todo = [(n, m) for n in range(2) for m in range(NG // mrows)]
    for u, (n, m) in enumerate(todo):
        if u >= slots:
            for s in range(4):
                out_copy(u - slots, s).wait()
        obuf[u % slots] = dot(left_ref[m * mrows:(m + 1) * mrows, :], right[:, n * 512:(n + 1) * 512])
        for s in range(4):
            out_copy(u, s).start()
    for u in range(len(todo) - slots, len(todo)):
        for s in range(4):
            out_copy(u, s).wait()
    for s in range(8):
        amp_copy(s).wait()


def spread(*operands):
    dma = pltpu.SemaphoreType.DMA
    return pl.pallas_call(
        spread_kernel,
        out_shape=(jax.ShapeDtypeStruct((NCH, 8, 128), f32), jax.ShapeDtypeStruct((NG, 8, 128), f32)),
        in_specs=[VM] * 6,
        out_specs=(ANY, ANY),
        scratch_shapes=[pltpu.VMEM((3 * NCH, 1024), bf16), pltpu.VMEM((NCH, 1024), f32), pltpu.VMEM((4, 512, 512), f32),
                        dma((8,)), dma((4, 4))],
        compiler_params=pltpu.CompilerParams(vmem_limit_bytes=20 * 2**20),
        cost_estimate=pl.CostEstimate(flops=3 * 2 * NG * NCH * 1024, bytes_accessed=12 * 2**20, transcendentals=0),
        name="spread",
    )(*operands)


def shards(surface_rows, he_states, energies, state_phase, momentum_phase, bessel_value, bessel_slope,
           channel_l2, surface_list, previous, coupling):
    prev = previous.reshape(NCH, 2, 2, 2, 128).transpose(0, 1, 3, 2, 4).reshape(NCH, 8, 128)
    ready = exchange(surface_rows.reshape(1792, 128), he_states.reshape(4, 2, 32, 128), surface_list, energies, state_phase,
                     momentum_phase.reshape(1, 256), bessel_value, bessel_slope, channel_l2.reshape(7, 128), prev, coupling)
    amplitudes, spectrum = spread(*ready)

    def whole(a):
        return a.reshape(-1, 2, 2, 2, 128).transpose(0, 1, 3, 2, 4).reshape(-1, 2, 2, 256)

    return whole(amplitudes), whole(spectrum)


def solution(mesh):
    split = P(None, ("row", "ch"), None, None)
    return jax.shard_map(
        shards,
        mesh=mesh,
        in_specs=(P(None, None, "ch", "row"), P(None, "row"), P(), P(), P(), P(), P(), P(), P("ch"), split, P()),
        out_specs=(split, split),
        check_vma=False,
    )
```

```python
import jax
import jax.numpy as jnp
from jax import lax
from jax.experimental import pallas as pl
from jax.experimental.pallas import tpu as pltpu
from jax.sharding import PartitionSpec as P

f32, bf16, i32 = jnp.float32, jnp.bfloat16, jnp.int32
time_step, momentum_top = 0.4, 2.0
NCH, NG = 896, 2048
HALF = 896
PART = 256
ANY = pl.BlockSpec(memory_space=pl.ANY)
VM = pl.BlockSpec(memory_space=pltpu.VMEM)
HBM = pl.BlockSpec(memory_space=pltpu.HBM)
MESH = pl.DeviceIdType.MESH
NT = (((1,), (1,)), ((), ()))


def split2(x):
    hi = x.astype(bf16).astype(f32)
    return hi, x - hi


def dot(a, b):
    return lax.dot_general(a, b, (((1,), (0,)), ((), ())), preferred_element_type=f32)


def exchange_kernel(surf_hbm, he_hbm, list_hbm, energy_hbm, phase_hbm, mp_hbm, bv_hbm, bs_hbm, lev_hbm, prev_hbm,
                    coup_hbm, left_ref, right_ref, first_ref, amp_ref,
                    own_s, he_v, list_ref, energy_ref, phase_ref, mp_v, bv_v, bs_v, lev_v, stage, other, own, got, rel, fromx, ybuf, own_list, lists, z_ref, hot_ref, bt_ref, fact_ref,
                    prev_ref, right_first, load_sem, prev_sem, coup_sem, core_send, core_recv, rel_send, rel_recv,
                    dir_send, dir_recv, comb_send, comb_recv, out_send, out_recv, list_send, list_recv):
    row, ch = lax.axis_index("row"), lax.axis_index("ch")
    x, core = row // 2, row % 2
    right, left, across = (x + 1) % 4, (x + 3) % 4, (x + 2) % 4
    partner = {"row": 2 * x + 1 - core}
    to_right, to_left = {"row": 2 * right + core}, {"row": 2 * left + core}

    loads = [pltpu.make_async_copy(src, dst, load_sem.at[k]) for k, (src, dst) in enumerate((
        (he_hbm, he_v), (surf_hbm, own_s), (list_hbm, list_ref), (energy_hbm, energy_ref), (phase_hbm, phase_ref),
        (mp_hbm, mp_v), (bv_hbm, bv_v), (bs_hbm, bs_v), (lev_hbm, lev_v)))]
    for load in loads:
        load.start()
    barrier = pltpu.get_barrier_semaphore()
    for target in (partner, to_right, to_left):
        pl.semaphore_signal(barrier, inc=1, device_id=target, device_id_type=MESH)
    for d in range(1, 16):
        pl.semaphore_signal(barrier, inc=1, device_id={"ch": (ch + d) % 16}, device_id_type=MESH)

    def coup_copy(k):
        return pltpu.make_async_copy(coup_hbm.at[pl.ds(k * PART, PART)], stage.at[k % 2], coup_sem.at[k % 2])

    prev_copies = [pltpu.make_async_copy(prev_hbm.at[:, s, :], prev_ref.at[:, pl.ds(s * 128, 128)], prev_sem.at[s])
                   for s in range(8)]

    loads[0].wait()
    parts = []
    for side in (1 - core, core):
        for n in range(2):
            for xx in range(4):
                parts.append(he_v[xx, side, pl.ds(n, 16, stride=2), :])
    he = jnp.concatenate(parts, axis=0)
    h_hi, h_lo = split2(he)
    h_left = jnp.concatenate([h_hi, h_hi, h_lo], axis=1).astype(bf16)
    loads[1].wait()
    for k in range(2):
        coup_copy(k).start()
    for copy in prev_copies:
        copy.start()
    for jc in range(7):
        rows = jnp.concatenate([own_s[pl.ds(jc * 8 + j, 32, stride=56), :] for j in range(8)], axis=0)
        s_hi, s_lo = split2(rows)
        s_right = jnp.concatenate([s_hi, s_lo, s_hi], axis=1).astype(bf16)
        part = lax.dot_general(h_left, s_right, NT, preferred_element_type=f32)
        lanes = slice(jc * 256, (jc + 1) * 256)
        for n in range(2):
            for xx in range(4):
                at = (n * 4 + xx) * 16
                other[n, xx, :, lanes] = part[at:at + 16]
                own[n, xx, :, lanes] = part[128 + at:144 + at]

    place = lax.broadcasted_iota(i32, (16, 128), 0) * 4 + lax.broadcasted_iota(i32, (16, 128), 1) // 32
    listed = jnp.full((16, 128), -1, i32)
    loads[2].wait()
    for j in range(56):
        listed = jnp.where(place == j, list_ref[j], listed)
    own_list[...] = listed
    pl.semaphore_wait(barrier, 18)

    def remote(src, dst, send, recv, target):
        return pltpu.make_async_remote_copy(src_ref=src, dst_ref=dst, send_sem=send, recv_sem=recv,
                                            device_id=target, device_id_type=MESH)

    def core_copy(n, k):
        block = (across, right, left, x)[k]
        return remote(other.at[n, block], got.at[n, block], core_send.at[n, k], core_recv.at[n, k], partner)

    for n, k in ((0, 0), (0, 1), (0, 2), (1, 0), (1, 1), (1, 2), (0, 3), (1, 3)):
        core_copy(n, k).start()
    here = pl.ds(pl.multiple_of(ch * 16, 16), 16)
    list_copies = [remote(own_list, lists.at[here], list_send.at[d], list_recv.at[d], {"ch": (ch + d) % 16})
                   for d in range(1, 16)]
    halves = (pl.ds(0, HALF), pl.ds(HALF, HALF))

    def add_core(n, k):
        block = (across, right, left, x)[k]
        core_copy(n, k).wait()
        own[n, block] += got[n, block]

    def relay(n, h):
        return remote(own.at[n, across, :, halves[h]], rel.at[n, h], rel_send.at[n, h], rel_recv.at[n, h],
                      (to_right, to_left)[h])

    def direct(n, h):
        block = (left, right)[h]
        return remote(own.at[n, block, :, halves[h]], fromx.at[n, 1 - h, :, halves[h]], dir_send.at[n, h],
                      dir_recv.at[n, h], (to_left, to_right)[h])

    def comb(n, h):
        block = (right, left)[h]
        return remote(own.at[n, block, :, halves[h]], fromx.at[n, h, :, halves[h]], comb_send.at[n, h],
                      comb_recv.at[n, h], (to_right, to_left)[h])

    def out(n, d):
        peer = (ch + d) % 16
        return remote(ybuf.at[n, pl.ds(pl.multiple_of(peer * 16, 16), 16)], z_ref.at[n, here],
                      out_send.at[n, d], out_recv.at[n, d], {"ch": peer})

    def ring_begin(n):
        add_core(n, 0)
        for h in range(2):
            relay(n, h).start()
        for k, h in ((1, 1), (2, 0)):
            add_core(n, k)
            direct(n, h).start()

    def ring_pass(n):
        for h, block in ((0, right), (1, left)):
            relay(n, h).wait()
            own[n, block, :, halves[h]] += rel[n, h]
            comb(n, h).start()

    def ring_end(n):
        for h in range(2):
            direct(n, h).wait()
            comb(n, h).wait()
        for jhi in range(14):
            lanes = slice(jhi * 128, (jhi + 1) * 128)
            ybuf[n, pl.ds(jhi, 16, stride=16), :] = own[n, x, :, lanes] + (fromx[n, 0, :, lanes] + fromx[n, 1, :, lanes])
        for d in range(1, 16):
            out(n, d).start()
        z_ref[n, here] = ybuf[n, here]

    def phases():
        for load in loads[3:]:
            load.wait()
        momenta = (lax.broadcasted_iota(i32, (8, 256), 1).astype(f32) + 0.5) * (momentum_top / 256)
        times = lax.broadcasted_iota(i32, (8, 256), 0).astype(f32) * time_step
        z16 = jnp.zeros((16, 256), f32)
        first = (row * 16 + ch) * 2
        for n in range(2):
            angle = energy_ref[first + n] * times + 0.5 * times * (momenta * momenta) + (phase_ref[first + n] + mp_v[...])
            cos, sin = (0.5 * time_step) * jnp.cos(angle), (0.5 * time_step) * jnp.sin(angle)
            for khi in range(2):
                c, s = cos[:, khi * 128:(khi + 1) * 128], sin[:, khi * 128:(khi + 1) * 128]
                block = jnp.concatenate([jnp.concatenate([c, s], 1), jnp.concatenate([-s, c], 1)], 0)
                hi, lo = split2(block)
                for d in range(2):
                    rows = [p for piece in (hi, hi, lo, lo) for p in ((piece, z16), (z16, piece))[d]]
                    at = (khi * 2 + d) * 256
                    fact_ref[n, :, at:at + 256] = jnp.concatenate(rows, axis=0).astype(bf16)

    def tables():
        def three(table):
            a, rest = split2(table)
            b, rest = split2(rest)
            return jnp.concatenate([a, b, rest, jnp.zeros_like(a)], axis=0).astype(bf16)

        table = jnp.concatenate([three(bv_v[...]), three(bs_v[...])], axis=1)
        level_of = lax.broadcasted_iota(i32, (128, 128), 0)
        for i in range(7):
            chosen = (level_of % 32 == jnp.broadcast_to(lev_v[i:i + 1, :], (128, 128))) & (level_of < 96)
            bt_ref[i * 128:(i + 1) * 128, :] = dot(jnp.transpose(chosen.astype(f32)).astype(bf16), table)

    def places():
        for copy in list_copies:
            copy.wait()
        row_of = jnp.transpose(lists[...])
        for i in range(7):
            channel = lax.broadcasted_iota(i32, (128, 256), 0) + i * 128
            for jlo in range(4):
                match = channel == jnp.broadcast_to(row_of[jlo * 32:jlo * 32 + 1, :], (128, 256))
                hot_ref[i * 128:(i + 1) * 128, jlo * 256:(jlo + 1) * 256] = match.astype(f32).astype(bf16)

    def split_coupling(k):
        coup_copy(k).wait()

        def some(i, _):
            at = pl.multiple_of(i * 32, 32)
            c = stage[k % 2, pl.ds(at, 32), :]
            hi = c.astype(bf16)
            to = pl.ds(pl.multiple_of(k * PART + i * 32, 32), 32)
            left_ref[to, 0:NCH] = hi
            left_ref[to, NCH:2 * NCH] = (c - hi.astype(f32)).astype(bf16)
            left_ref[to, 2 * NCH:3 * NCH] = hi
            return 0

        lax.fori_loop(0, PART // 32, some, 0)
        if k + 2 < NG // PART:
            coup_copy(k + 2).start()

    def add_fresh(n, rights):
        for d in range(1, 16):
            out(n, d).wait()
        hi, lo = split2(z_ref[n])
        picks = []
        for jlo in range(4):
            pair = [a[:, jlo * 32:(jlo + 1) * 32] for a in (hi, lo)]
            picks.append(jnp.concatenate(pair + pair, axis=1).astype(bf16))
        picks = jnp.concatenate(picks, axis=0)
        for i in range(7):
            at = pl.ds(i * 128, 128)
            chosen = dot(hot_ref[at, :], picks).astype(bf16)
            sums = dot(chosen, fact_ref[n])
            for khi in range(2):
                value_at = bt_ref[at, khi * 128:(khi + 1) * 128]
                slope_at = bt_ref[at, 256 + khi * 128:256 + (khi + 1) * 128]
                for p in range(2):
                    col = khi * 512 + p * 128
                    fresh = value_at * sums[:, col + 256:col + 384] - slope_at * sums[:, col:col + 128]
                    cols = slice((khi * 2 + p) * 128, (khi * 2 + p + 1) * 128)
                    both = slice(n * 512 + (khi * 2 + p) * 128, n * 512 + (khi * 2 + p + 1) * 128)
                    total = prev_ref[at, both] + fresh
                    amp_ref[at, both] = total
                    high = total.astype(bf16)
                    rights[at, cols] = high
                    rights[pl.ds(NCH + i * 128, 128), cols] = high
                    rights[pl.ds(2 * NCH + i * 128, 128), cols] = (total - high.astype(f32)).astype(bf16)

    for n in range(2):
        for tail in (14, 15):
            ybuf[n, pl.ds(tail, 16, stride=16), :] = jnp.zeros((16, 128), f32)
    ring_begin(0)
    for copy in list_copies:
        copy.start()
    lists[here] = listed
    add_core(0, 3)
    phases()
    split_coupling(0)
    ring_pass(0)
    ring_begin(1)
    add_core(1, 3)
    tables()
    split_coupling(1)
    ring_end(0)
    split_coupling(2)
    ring_pass(1)
    places()
    for k in range(3, 8):
        split_coupling(k)
    for copy in prev_copies:
        copy.wait()
    add_fresh(0, right_first)
    ring_end(1)
    for m in range(2):
        first_ref[m * 1024:(m + 1) * 1024, :] = dot(left_ref[m * 1024:(m + 1) * 1024, :], right_first[...])
    add_fresh(1, right_ref)


def exchange(*operands):
    dma = pltpu.SemaphoreType.DMA
    block = pltpu.VMEM((2, 4, 16, 1792), f32)
    return pl.pallas_call(
        exchange_kernel,
        out_shape=(jax.ShapeDtypeStruct((NG, 3 * NCH), bf16), jax.ShapeDtypeStruct((3 * NCH, 512), bf16),
                   jax.ShapeDtypeStruct((NG, 512), f32), jax.ShapeDtypeStruct((NCH, 1024), f32)),
        in_specs=[HBM] * 11,
        out_specs=(VM,) * 4,
        scratch_shapes=[pltpu.VMEM((1792, 128), f32), pltpu.VMEM((4, 2, 32, 128), f32), pltpu.SMEM((56,), i32),
                        pltpu.SMEM((256,), f32), pltpu.SMEM((256,), f32), pltpu.VMEM((1, 256), f32),
                        pltpu.VMEM((32, 256), f32), pltpu.VMEM((32, 256), f32), pltpu.VMEM((7, 128), i32),
                        pltpu.VMEM((2, PART, NCH), f32), block, block, block,
                        pltpu.VMEM((2, 2, 16, HALF), f32), pltpu.VMEM((2, 2, 16, 1792), f32), pltpu.VMEM((2, 256, 128), f32),
                        pltpu.VMEM((16, 128), i32), pltpu.VMEM((256, 128), i32), pltpu.VMEM((2, 256, 128), f32),
                        pltpu.VMEM((NCH, 1024), bf16), pltpu.VMEM((NCH, 512), f32), pltpu.VMEM((2, 128, 1024), bf16),
                        pltpu.VMEM((NCH, 1024), f32), pltpu.VMEM((3 * NCH, 512), bf16),
                        dma((9,)), dma((8,)), dma((2,)), dma((2, 4)), dma((2, 4)), dma((2, 2)), dma((2, 2)),
                        dma((2, 2)), dma((2, 2)), dma((2, 2)), dma((2, 2)), dma((2, 16)), dma((2, 16)), dma((16,)), dma((16,))],
        compiler_params=pltpu.CompilerParams(vmem_limit_bytes=32 * 2**20, collective_id=0, has_side_effects=True),
        cost_estimate=pl.CostEstimate(flops=3 * NG * NCH * 1024, bytes_accessed=14 * 2**20, transcendentals=0),
        name="exchange",
    )(*(pltpu.with_memory_space_constraint(a, pltpu.HBM) for a in operands))


def spread_kernel(left_ref, right_ref, first_ref, amp_ref, amp_hbm, spec_hbm, obuf, asem, fsem, osem):
    bounds = (0, 1024, 1536, 1792, 2048)

    def amp_copy(s):
        return pltpu.make_async_copy(amp_ref.at[:, pl.ds(s * 128, 128)], amp_hbm.at[:, s, :], asem.at[s])

    def first_copy(s):
        return pltpu.make_async_copy(first_ref.at[:, pl.ds(s * 128, 128)], spec_hbm.at[:, s, :], fsem.at[s])

    def out_copy(m, s):
        at = pl.ds(bounds[m], bounds[m + 1] - bounds[m])
        return pltpu.make_async_copy(obuf.at[at, pl.ds(s * 128, 128)], spec_hbm.at[at, 4 + s, :], osem.at[m, s])

    for s in range(4):
        first_copy(s).start()
    for s in range(8):
        amp_copy(s).start()
    for m in range(4):
        at = pl.ds(bounds[m], bounds[m + 1] - bounds[m])
        obuf[at, :] = dot(left_ref[at, :], right_ref[...])
        for s in range(4):
            out_copy(m, s).start()
    for s in range(4):
        first_copy(s).wait()
    for s in range(8):
        amp_copy(s).wait()
    for m in range(4):
        for s in range(4):
            out_copy(m, s).wait()


def spread(*operands):
    dma = pltpu.SemaphoreType.DMA
    return pl.pallas_call(
        spread_kernel,
        out_shape=(jax.ShapeDtypeStruct((NCH, 8, 128), f32), jax.ShapeDtypeStruct((NG, 8, 128), f32)),
        in_specs=[VM] * 4,
        out_specs=(ANY, ANY),
        scratch_shapes=[pltpu.VMEM((NG, 512), f32), dma((8,)), dma((4,)), dma((4, 4))],
        compiler_params=pltpu.CompilerParams(vmem_limit_bytes=16 * 2**20),
        cost_estimate=pl.CostEstimate(flops=3 * NG * NCH * 1024, bytes_accessed=12 * 2**20, transcendentals=0),
        name="spread",
    )(*operands)


def shards(surface_rows, he_states, energies, state_phase, momentum_phase, bessel_value, bessel_slope,
           channel_l2, surface_list, previous, coupling):
    prev = previous.reshape(NCH, 2, 2, 2, 128).transpose(0, 1, 3, 2, 4).reshape(NCH, 8, 128)
    ready = exchange(surface_rows.reshape(1792, 128), he_states.reshape(4, 2, 32, 128), surface_list, energies, state_phase,
                     momentum_phase.reshape(1, 256), bessel_value, bessel_slope, channel_l2.reshape(7, 128), prev, coupling)
    amplitudes, spectrum = spread(*ready)

    def whole(a):
        return a.reshape(-1, 2, 2, 2, 128).transpose(0, 1, 3, 2, 4).reshape(-1, 2, 2, 256)

    return whole(amplitudes), whole(spectrum)


def solution(mesh):
    split = P(None, ("row", "ch"), None, None)
    return jax.shard_map(
        shards,
        mesh=mesh,
        in_specs=(P(None, None, "ch", "row"), P(None, "row"), P(), P(), P(), P(), P(), P(), P("ch"), split, P()),
        out_specs=(split, split),
        check_vma=False,
    )
```

```python
import jax
import jax.numpy as jnp
from jax import lax
from jax.experimental import pallas as pl
from jax.experimental.pallas import tpu as pltpu
from jax.sharding import PartitionSpec as P

f32, bf16, i32 = jnp.float32, jnp.bfloat16, jnp.int32
time_step, momentum_top = 0.4, 2.0
NCH, NG = 896, 2048
HALF = 896
PART = 256
STEP = 448
ANY = pl.BlockSpec(memory_space=pl.ANY)
VM = pl.BlockSpec(memory_space=pltpu.VMEM)
HBM = pl.BlockSpec(memory_space=pltpu.HBM)
MESH = pl.DeviceIdType.MESH
NT = (((1,), (1,)), ((), ()))


def split2(x):
    hi = x.astype(bf16).astype(f32)
    return hi, x - hi


def dot(a, b):
    return lax.dot_general(a, b, (((1,), (0,)), ((), ())), preferred_element_type=f32)


def exchange_kernel(surf_hbm, he_hbm, list_hbm, energy_hbm, phase_hbm, mp_hbm, bv_hbm, bs_hbm, lev_hbm, prev_hbm,
                    coup_hbm, left_ref, right_ref, first_ref, amp_ref,
                    own_s, he_v, list_ref, energy_ref, phase_ref, mp_v, bv_v, bs_v, lev_v, stage, other, own, got, rel, fromx, ybuf, own_list, lists, z_ref, hot_ref, mask_ref, bt_ref, fact_ref,
                    prev_ref, right_first, load_sem, prev_sem, coup_sem, core_send, core_recv, rel_send, rel_recv,
                    dir_send, dir_recv, comb_send, comb_recv, out_send, out_recv, list_send, list_recv):
    row, ch = lax.axis_index("row"), lax.axis_index("ch")
    x, core = row // 2, row % 2
    right, left, across = (x + 1) % 4, (x + 3) % 4, (x + 2) % 4
    partner = {"row": 2 * x + 1 - core}
    to_right, to_left = {"row": 2 * right + core}, {"row": 2 * left + core}

    loads = [pltpu.make_async_copy(src, dst, load_sem.at[k]) for k, (src, dst) in enumerate((
        (surf_hbm, own_s), (he_hbm, he_v), (list_hbm, list_ref), (energy_hbm, energy_ref), (phase_hbm, phase_ref),
        (mp_hbm, mp_v), (bv_hbm, bv_v), (bs_hbm, bs_v), (lev_hbm, lev_v)))]
    for load in loads[:2]:
        load.start()
    barrier = pltpu.get_barrier_semaphore()
    for target in (partner, to_right, to_left):
        pl.semaphore_signal(barrier, inc=1, device_id=target, device_id_type=MESH)
    for d in range(1, 16):
        pl.semaphore_signal(barrier, inc=1, device_id={"ch": (ch + d) % 16}, device_id_type=MESH)

    def coup_copy(k):
        return pltpu.make_async_copy(coup_hbm.at[pl.ds(k * PART, PART)], stage.at[k % 2], coup_sem.at[k % 2])

    prev_copies = [pltpu.make_async_copy(prev_hbm.at[:, s, :], prev_ref.at[:, pl.ds(s * 128, 128)], prev_sem.at[s])
                   for s in range(8)]

    loads[1].wait()
    parts = []
    for side in (1 - core, core):
        for n in range(2):
            for xx in range(4):
                parts.append(he_v[xx, side, pl.ds(n, 16, stride=2), :])
    he = jnp.concatenate(parts, axis=0)
    h_hi, h_lo = split2(he)
    h_left = jnp.concatenate([h_hi, h_hi, h_lo], axis=1).astype(bf16)
    loads[0].wait()
    for jc in range(7):
        rows = jnp.concatenate([own_s[pl.ds(jc * 8 + j, 32, stride=56), :] for j in range(8)], axis=0)
        s_hi, s_lo = split2(rows)
        s_right = jnp.concatenate([s_hi, s_lo, s_hi], axis=1).astype(bf16)
        part = lax.dot_general(h_left, s_right, NT, preferred_element_type=f32)
        lanes = slice(jc * 256, (jc + 1) * 256)
        for n in range(2):
            for xx in range(4):
                at = (n * 4 + xx) * 16
                other[n, xx, :, lanes] = part[at:at + 16]
                own[n, xx, :, lanes] = part[128 + at:144 + at]

    pl.semaphore_wait(barrier, 18)

    def remote(src, dst, send, recv, target):
        return pltpu.make_async_remote_copy(src_ref=src, dst_ref=dst, send_sem=send, recv_sem=recv,
                                            device_id=target, device_id_type=MESH)

    def core_copy(n, k):
        block = (across, right, left, x)[k]
        return remote(other.at[n, block], got.at[n, block], core_send.at[n, k], core_recv.at[n, k], partner)

    for k in range(3):
        core_copy(0, k).start()
    for load in loads[2:]:
        load.start()
    place = lax.broadcasted_iota(i32, (16, 128), 0) * 4 + lax.broadcasted_iota(i32, (16, 128), 1) // 32
    listed = jnp.full((16, 128), -1, i32)
    loads[2].wait()
    for j in range(56):
        listed = jnp.where(place == j, list_ref[j], listed)
    own_list[...] = listed
    here = pl.ds(pl.multiple_of(ch * 16, 16), 16)
    list_copies = [remote(own_list, lists.at[here], list_send.at[d], list_recv.at[d], {"ch": (ch + d) % 16})
                   for d in range(1, 16)]
    halves = (pl.ds(0, HALF), pl.ds(HALF, HALF))

    def add_core(n, k):
        block = (across, right, left, x)[k]
        core_copy(n, k).wait()
        own[n, block] += got[n, block]

    def relay(n, h):
        return remote(own.at[n, across, :, halves[h]], rel.at[n, h], rel_send.at[n, h], rel_recv.at[n, h],
                      (to_right, to_left)[h])

    def direct(n, h):
        block = (left, right)[h]
        return remote(own.at[n, block, :, halves[h]], fromx.at[n, 1 - h, :, halves[h]], dir_send.at[n, h],
                      dir_recv.at[n, h], (to_left, to_right)[h])

    def comb(n, h):
        block = (right, left)[h]
        return remote(own.at[n, block, :, halves[h]], fromx.at[n, h, :, halves[h]], comb_send.at[n, h],
                      comb_recv.at[n, h], (to_right, to_left)[h])

    def out(n, d):
        peer = (ch + d) % 16
        return remote(ybuf.at[n, pl.ds(pl.multiple_of(peer * 16, 16), 16)], z_ref.at[n, here],
                      out_send.at[n, d], out_recv.at[n, d], {"ch": peer})

    def ring_begin(n):
        add_core(n, 0)
        for h in range(2):
            relay(n, h).start()
        for k, h in ((1, 1), (2, 0)):
            add_core(n, k)
            direct(n, h).start()

    def ring_pass(n):
        for h, block in ((0, right), (1, left)):
            relay(n, h).wait()
            own[n, block, :, halves[h]] += rel[n, h]
            comb(n, h).start()

    def ring_end(n):
        for h in range(2):
            direct(n, h).wait()
            comb(n, h).wait()
        for jhi in range(14):
            lanes = slice(jhi * 128, (jhi + 1) * 128)
            ybuf[n, pl.ds(jhi, 16, stride=16), :] = own[n, x, :, lanes] + (fromx[n, 0, :, lanes] + fromx[n, 1, :, lanes])
        for d in range(1, 16):
            out(n, d).start()
        z_ref[n, here] = ybuf[n, here]

    def phases():
        for load in loads[3:]:
            load.wait()
        momenta = (lax.broadcasted_iota(i32, (8, 256), 1).astype(f32) + 0.5) * (momentum_top / 256)
        times = lax.broadcasted_iota(i32, (8, 256), 0).astype(f32) * time_step
        z16 = jnp.zeros((16, 256), f32)
        first = (row * 16 + ch) * 2
        for n in range(2):
            angle = energy_ref[first + n] * times + 0.5 * times * (momenta * momenta) + (phase_ref[first + n] + mp_v[...])
            cos, sin = (0.5 * time_step) * jnp.cos(angle), (0.5 * time_step) * jnp.sin(angle)
            for khi in range(2):
                c, s = cos[:, khi * 128:(khi + 1) * 128], sin[:, khi * 128:(khi + 1) * 128]
                block = jnp.concatenate([jnp.concatenate([c, s], 1), jnp.concatenate([-s, c], 1)], 0)
                hi, lo = split2(block)
                for d in range(2):
                    rows = [p for piece in (hi,) * 4 + (lo,) * 4 for p in ((piece, z16), (z16, piece))[d]]
                    at = (khi * 2 + d) * 256
                    fact_ref[n, :, at:at + 256] = jnp.concatenate(rows, axis=0).astype(bf16)

    def tables():
        def three(table):
            a, rest = split2(table)
            b, rest = split2(rest)
            return jnp.concatenate([a, b, rest, jnp.zeros_like(a)], axis=0).astype(bf16)

        table = jnp.concatenate([three(bv_v[...]), three(bs_v[...])], axis=1)
        level_of = lax.broadcasted_iota(i32, (128, 128), 0)
        for i in range(7):
            chosen = (level_of % 32 == jnp.broadcast_to(lev_v[i:i + 1, :], (128, 128))) & (level_of < 96)
            bt_ref[i * 128:(i + 1) * 128, :] = dot(jnp.transpose(chosen.astype(f32)).astype(bf16), table)

    def places():
        for copy in list_copies:
            copy.wait()
        all_lists = lists[...]
        row_of = jnp.transpose(all_lists)
        numbers = all_lists.astype(f32)
        wide = jnp.concatenate([numbers[:, j // 2 * 32:j // 2 * 32 + 32] for j in range(8)], axis=1)
        number_hi, number_lo = (piece.astype(bf16) for piece in split2(wide))
        for i in range(7):
            at = slice(i * 128, (i + 1) * 128)
            channel = lax.broadcasted_iota(i32, (128, 256), 0) + i * 128
            match = channel == jnp.broadcast_to(row_of[0:1, :], (128, 256))
            for jlo in range(1, 4):
                match = match | (channel == jnp.broadcast_to(row_of[jlo * 32:jlo * 32 + 1, :], (128, 256)))
            hot = match.astype(f32).astype(bf16)
            hot_ref[at, :] = hot
            mask_ref[at, :] = (dot(hot, number_hi) + dot(hot, number_lo) == channel.astype(f32)).astype(f32)

    def split_coupling(k):
        coup_copy(k).wait()

        def some(i, _):
            at = pl.multiple_of(i * 32, 32)
            c = stage[k % 2, pl.ds(at, 32), :]
            hi = c.astype(bf16)
            to = pl.ds(pl.multiple_of(k * PART + i * 32, 32), 32)
            left_ref[to, 0:NCH] = hi
            left_ref[to, NCH:2 * NCH] = (c - hi.astype(f32)).astype(bf16)
            left_ref[to, 2 * NCH:3 * NCH] = hi
            return 0

        lax.fori_loop(0, PART // 32, some, 0)
        if k + 2 < NG // PART:
            coup_copy(k + 2).start()

    def add_fresh(n, rights):
        for d in range(1, 16):
            out(n, d).wait()
        hi, lo = split2(z_ref[n])
        picks = jnp.concatenate([a[:, jlo * 32:(jlo + 1) * 32] for jlo in range(4) for a in (hi, lo)], axis=1).astype(bf16)
        for i in range(NCH // STEP):
            at = pl.ds(i * STEP, STEP)
            four = dot(hot_ref[at, :], picks) * mask_ref[at, :]
            two = four[:, :128] + four[:, 128:]
            sums = dot(jnp.concatenate([two, two], axis=1).astype(bf16), fact_ref[n])
            for khi in range(2):
                value_at = bt_ref[at, khi * 128:(khi + 1) * 128]
                slope_at = bt_ref[at, 256 + khi * 128:256 + (khi + 1) * 128]
                for p in range(2):
                    col = khi * 512 + p * 128
                    fresh = value_at * sums[:, col + 256:col + 384] - slope_at * sums[:, col:col + 128]
                    cols = slice((khi * 2 + p) * 128, (khi * 2 + p + 1) * 128)
                    both = slice(n * 512 + (khi * 2 + p) * 128, n * 512 + (khi * 2 + p + 1) * 128)
                    total = prev_ref[at, both] + fresh
                    amp_ref[at, both] = total
                    high = total.astype(bf16)
                    rights[at, cols] = high
                    rights[pl.ds(NCH + i * STEP, STEP), cols] = high
                    rights[pl.ds(2 * NCH + i * STEP, STEP), cols] = (total - high.astype(f32)).astype(bf16)

    for n in range(2):
        for tail in (14, 15):
            ybuf[n, pl.ds(tail, 16, stride=16), :] = jnp.zeros((16, 128), f32)
    ring_begin(0)
    for n, k in ((0, 3), (1, 0), (1, 1), (1, 2), (1, 3)):
        core_copy(n, k).start()
    for copy in list_copies:
        copy.start()
    lists[here] = listed
    for k in range(2):
        coup_copy(k).start()
    for copy in prev_copies:
        copy.start()
    add_core(0, 3)
    phases()
    split_coupling(0)
    ring_pass(0)
    ring_begin(1)
    add_core(1, 3)
    tables()
    split_coupling(1)
    ring_end(0)
    split_coupling(2)
    ring_pass(1)
    places()
    for k in range(3, 8):
        split_coupling(k)
    for copy in prev_copies:
        copy.wait()
    add_fresh(0, right_first)
    ring_end(1)
    for m in range(2):
        first_ref[m * 1024:(m + 1) * 1024, :] = dot(left_ref[m * 1024:(m + 1) * 1024, :], right_first[...])
    add_fresh(1, right_ref)


def exchange(*operands):
    dma = pltpu.SemaphoreType.DMA
    block = pltpu.VMEM((2, 4, 16, 1792), f32)
    return pl.pallas_call(
        exchange_kernel,
        out_shape=(jax.ShapeDtypeStruct((NG, 3 * NCH), bf16), jax.ShapeDtypeStruct((3 * NCH, 512), bf16),
                   jax.ShapeDtypeStruct((NG, 512), f32), jax.ShapeDtypeStruct((NCH, 1024), f32)),
        in_specs=[HBM] * 11,
        out_specs=(VM,) * 4,
        scratch_shapes=[pltpu.VMEM((1792, 128), f32), pltpu.VMEM((4, 2, 32, 128), f32), pltpu.SMEM((56,), i32),
                        pltpu.SMEM((256,), f32), pltpu.SMEM((256,), f32), pltpu.VMEM((1, 256), f32),
                        pltpu.VMEM((32, 256), f32), pltpu.VMEM((32, 256), f32), pltpu.VMEM((7, 128), i32),
                        pltpu.VMEM((2, PART, NCH), f32), block, block, block,
                        pltpu.VMEM((2, 2, 16, HALF), f32), pltpu.VMEM((2, 2, 16, 1792), f32), pltpu.VMEM((2, 256, 128), f32),
                        pltpu.VMEM((16, 128), i32), pltpu.VMEM((256, 128), i32), pltpu.VMEM((2, 256, 128), f32),
                        pltpu.VMEM((NCH, 256), bf16), pltpu.VMEM((NCH, 256), f32), pltpu.VMEM((NCH, 512), f32),
                        pltpu.VMEM((2, 256, 1024), bf16),
                        pltpu.VMEM((NCH, 1024), f32), pltpu.VMEM((3 * NCH, 512), bf16),
                        dma((9,)), dma((8,)), dma((2,)), dma((2, 4)), dma((2, 4)), dma((2, 2)), dma((2, 2)),
                        dma((2, 2)), dma((2, 2)), dma((2, 2)), dma((2, 2)), dma((2, 16)), dma((2, 16)), dma((16,)), dma((16,))],
        compiler_params=pltpu.CompilerParams(vmem_limit_bytes=32 * 2**20, collective_id=0, has_side_effects=True),
        cost_estimate=pl.CostEstimate(flops=3 * NG * NCH * 1024, bytes_accessed=14 * 2**20, transcendentals=0),
        name="exchange",
    )(*(pltpu.with_memory_space_constraint(a, pltpu.HBM) for a in operands))


def spread_kernel(left_ref, right_ref, first_ref, amp_ref, amp_hbm, spec_hbm, obuf, asem, fsem, osem):
    bounds = (0, 1024, 1536, 1792, 2048)

    def amp_copy(s):
        return pltpu.make_async_copy(amp_ref.at[:, pl.ds(s * 128, 128)], amp_hbm.at[:, s, :], asem.at[s])

    def first_copy(s):
        return pltpu.make_async_copy(first_ref.at[:, pl.ds(s * 128, 128)], spec_hbm.at[:, s, :], fsem.at[s])

    def out_copy(m, s):
        at = pl.ds(bounds[m], bounds[m + 1] - bounds[m])
        return pltpu.make_async_copy(obuf.at[at, pl.ds(s * 128, 128)], spec_hbm.at[at, 4 + s, :], osem.at[m, s])

    for s in range(4):
        first_copy(s).start()
    for s in range(8):
        amp_copy(s).start()
    for m in range(4):
        at = pl.ds(bounds[m], bounds[m + 1] - bounds[m])
        obuf[at, :] = dot(left_ref[at, :], right_ref[...])
        for s in range(4):
            out_copy(m, s).start()
    for s in range(4):
        first_copy(s).wait()
    for s in range(8):
        amp_copy(s).wait()
    for m in range(4):
        for s in range(4):
            out_copy(m, s).wait()


def spread(*operands):
    dma = pltpu.SemaphoreType.DMA
    return pl.pallas_call(
        spread_kernel,
        out_shape=(jax.ShapeDtypeStruct((NCH, 8, 128), f32), jax.ShapeDtypeStruct((NG, 8, 128), f32)),
        in_specs=[VM] * 4,
        out_specs=(ANY, ANY),
        scratch_shapes=[pltpu.VMEM((NG, 512), f32), dma((8,)), dma((4,)), dma((4, 4))],
        compiler_params=pltpu.CompilerParams(vmem_limit_bytes=16 * 2**20),
        cost_estimate=pl.CostEstimate(flops=3 * NG * NCH * 1024, bytes_accessed=12 * 2**20, transcendentals=0),
        name="spread",
    )(*operands)


def shards(surface_rows, he_states, energies, state_phase, momentum_phase, bessel_value, bessel_slope,
           channel_l2, surface_list, previous, coupling):
    prev = previous.reshape(NCH, 2, 2, 2, 128).transpose(0, 1, 3, 2, 4).reshape(NCH, 8, 128)
    ready = exchange(surface_rows.reshape(1792, 128), he_states.reshape(4, 2, 32, 128), surface_list, energies, state_phase,
                     momentum_phase.reshape(1, 256), bessel_value, bessel_slope, channel_l2.reshape(7, 128), prev, coupling)
    amplitudes, spectrum = spread(*ready)

    def whole(a):
        return a.reshape(-1, 2, 2, 2, 128).transpose(0, 1, 3, 2, 4).reshape(-1, 2, 2, 256)

    return whole(amplitudes), whole(spectrum)


def solution(mesh):
    split = P(None, ("row", "ch"), None, None)
    return jax.shard_map(
        shards,
        mesh=mesh,
        in_specs=(P(None, None, "ch", "row"), P(None, "row"), P(), P(), P(), P(), P(), P(), P("ch"), split, P()),
        out_specs=(split, split),
        check_vma=False,
    )
```

```python
import jax
import jax.numpy as jnp
from jax import lax
from jax.experimental import pallas as pl
from jax.experimental.pallas import tpu as pltpu
from jax.sharding import PartitionSpec as P

f32, bf16, i32 = jnp.float32, jnp.bfloat16, jnp.int32
time_step, momentum_top = 0.4, 2.0
NCH, NG = 896, 2048
HALF = 896
PART = 256
STEP = 448
ANY = pl.BlockSpec(memory_space=pl.ANY)
VM = pl.BlockSpec(memory_space=pltpu.VMEM)
HBM = pl.BlockSpec(memory_space=pltpu.HBM)
MESH = pl.DeviceIdType.MESH
NT = (((1,), (1,)), ((), ()))
OFFSETS = sorted(range(1, 16), key=lambda d: -min(d // 4, 4 - d // 4) - min(d % 4, 4 - d % 4))


def split2(x):
    hi = x.astype(bf16).astype(f32)
    return hi, x - hi


def dot(a, b):
    return lax.dot_general(a, b, (((1,), (0,)), ((), ())), preferred_element_type=f32)


def exchange_kernel(surf_hbm, he_hbm, list_hbm, energy_hbm, phase_hbm, mp_hbm, bv_hbm, bs_hbm, lev_hbm, prev_hbm,
                    coup_hbm, left_ref, right_ref, first_ref, amp_ref,
                    own_s, he_v, list_ref, energy_ref, phase_ref, mp_v, bv_v, bs_v, lev_v, stage, other, own, got, rel, fromx, ybuf, own_list, lists, z_ref, hot_ref, mask_ref, bt_ref, fact_ref,
                    prev_ref, right_first, load_sem, prev_sem, coup_sem, core_send, core_recv, rel_send, rel_recv,
                    dir_send, dir_recv, comb_send, comb_recv, out_send, out_recv, list_send, list_recv):
    row, ch = lax.axis_index("row"), lax.axis_index("ch")
    x, core = row // 2, row % 2
    right, left, across = (x + 1) % 4, (x + 3) % 4, (x + 2) % 4
    partner = {"row": 2 * x + 1 - core}
    to_right, to_left = {"row": 2 * right + core}, {"row": 2 * left + core}

    loads = [pltpu.make_async_copy(src, dst, load_sem.at[k]) for k, (src, dst) in enumerate((
        (surf_hbm, own_s), (he_hbm, he_v), (list_hbm, list_ref), (energy_hbm, energy_ref), (phase_hbm, phase_ref),
        (mp_hbm, mp_v), (bv_hbm, bv_v), (bs_hbm, bs_v), (lev_hbm, lev_v)))]
    for load in loads[:2]:
        load.start()
    barrier = pltpu.get_barrier_semaphore()
    for target in (partner, to_right, to_left):
        pl.semaphore_signal(barrier, inc=1, device_id=target, device_id_type=MESH)
    for d in range(1, 16):
        pl.semaphore_signal(barrier, inc=1, device_id={"ch": (ch + d) % 16}, device_id_type=MESH)

    def coup_copy(k):
        return pltpu.make_async_copy(coup_hbm.at[pl.ds(k * PART, PART)], stage.at[k % 2], coup_sem.at[k % 2])

    prev_copies = [pltpu.make_async_copy(prev_hbm.at[:, s, :], prev_ref.at[:, pl.ds(s * 128, 128)], prev_sem.at[s])
                   for s in range(8)]

    loads[1].wait()
    parts = []
    for side in (1 - core, core):
        for n in range(2):
            for xx in range(4):
                parts.append(he_v[xx, side, pl.ds(n, 16, stride=2), :])
    he = jnp.concatenate(parts, axis=0)
    h_hi, h_lo = split2(he)
    h_left = jnp.concatenate([h_hi, h_hi, h_lo], axis=1).astype(bf16)
    loads[0].wait()
    for jc in range(7):
        rows = jnp.concatenate([own_s[pl.ds(jc * 8 + j, 32, stride=56), :] for j in range(8)], axis=0)
        s_hi, s_lo = split2(rows)
        s_right = jnp.concatenate([s_hi, s_lo, s_hi], axis=1).astype(bf16)
        part = lax.dot_general(h_left, s_right, NT, preferred_element_type=f32)
        lanes = slice(jc * 256, (jc + 1) * 256)
        for n in range(2):
            for xx in range(4):
                at = (n * 4 + xx) * 16
                other[n, xx, :, lanes] = part[at:at + 16]
                own[n, xx, :, lanes] = part[128 + at:144 + at]

    pl.semaphore_wait(barrier, 18)

    def remote(src, dst, send, recv, target):
        return pltpu.make_async_remote_copy(src_ref=src, dst_ref=dst, send_sem=send, recv_sem=recv,
                                            device_id=target, device_id_type=MESH)

    def core_copy(n, k):
        block = (across, right, left, x)[k]
        return remote(other.at[n, block], got.at[n, block], core_send.at[n, k], core_recv.at[n, k], partner)

    for k in range(3):
        core_copy(0, k).start()
    for load in loads[2:]:
        load.start()
    place = lax.broadcasted_iota(i32, (16, 128), 0) * 4 + lax.broadcasted_iota(i32, (16, 128), 1) // 32
    listed = jnp.full((16, 128), -1, i32)
    loads[2].wait()
    for j in range(56):
        listed = jnp.where(place == j, list_ref[j], listed)
    own_list[...] = listed
    here = pl.ds(pl.multiple_of(ch * 16, 16), 16)
    list_copies = [remote(own_list, lists.at[here], list_send.at[d], list_recv.at[d], {"ch": (ch + d) % 16})
                   for d in range(1, 16)]
    halves = (pl.ds(0, HALF), pl.ds(HALF, HALF))

    def add_core(n, k):
        block = (across, right, left, x)[k]
        core_copy(n, k).wait()
        own[n, block] += got[n, block]

    def relay(n, h):
        return remote(own.at[n, across, :, halves[h]], rel.at[n, h], rel_send.at[n, h], rel_recv.at[n, h],
                      (to_right, to_left)[h])

    def direct(n, h):
        block = (left, right)[h]
        return remote(own.at[n, block, :, halves[h]], fromx.at[n, 1 - h, :, halves[h]], dir_send.at[n, h],
                      dir_recv.at[n, h], (to_left, to_right)[h])

    def comb(n, h):
        block = (right, left)[h]
        return remote(own.at[n, block, :, halves[h]], fromx.at[n, h, :, halves[h]], comb_send.at[n, h],
                      comb_recv.at[n, h], (to_right, to_left)[h])

    def out(n, d):
        peer = (ch // 4 + d // 4) % 4 * 4 + (ch % 4 + d % 4) % 4
        return remote(ybuf.at[n, pl.ds(pl.multiple_of(peer * 16, 16), 16)], z_ref.at[n, here],
                      out_send.at[n, d], out_recv.at[n, d], {"ch": peer})

    def ring_begin(n):
        add_core(n, 0)
        for h in range(2):
            relay(n, h).start()
        for k, h in ((1, 1), (2, 0)):
            add_core(n, k)
            direct(n, h).start()

    def ring_pass(n):
        for h, block in ((0, right), (1, left)):
            relay(n, h).wait()
            own[n, block, :, halves[h]] += rel[n, h]
            comb(n, h).start()

    def ring_end(n):
        for h in range(2):
            direct(n, h).wait()
            comb(n, h).wait()
        for jhi in range(14):
            lanes = slice(jhi * 128, (jhi + 1) * 128)
            ybuf[n, pl.ds(jhi, 16, stride=16), :] = own[n, x, :, lanes] + (fromx[n, 0, :, lanes] + fromx[n, 1, :, lanes])
        for d in OFFSETS:
            out(n, d).start()
        z_ref[n, here] = ybuf[n, here]

    def phases():
        for load in loads[3:]:
            load.wait()
        momenta = (lax.broadcasted_iota(i32, (8, 256), 1).astype(f32) + 0.5) * (momentum_top / 256)
        times = lax.broadcasted_iota(i32, (8, 256), 0).astype(f32) * time_step
        z16 = jnp.zeros((16, 256), f32)
        first = (row * 16 + ch) * 2
        for n in range(2):
            angle = energy_ref[first + n] * times + 0.5 * times * (momenta * momenta) + (phase_ref[first + n] + mp_v[...])
            cos, sin = (0.5 * time_step) * jnp.cos(angle), (0.5 * time_step) * jnp.sin(angle)
            for khi in range(2):
                c, s = cos[:, khi * 128:(khi + 1) * 128], sin[:, khi * 128:(khi + 1) * 128]
                block = jnp.concatenate([jnp.concatenate([c, s], 1), jnp.concatenate([-s, c], 1)], 0)
                hi, lo = split2(block)
                for d in range(2):
                    rows = [p for piece in (hi,) * 4 + (lo,) * 4 for p in ((piece, z16), (z16, piece))[d]]
                    at = (khi * 2 + d) * 256
                    fact_ref[n, :, at:at + 256] = jnp.concatenate(rows, axis=0).astype(bf16)

    def tables():
        def three(table):
            a, rest = split2(table)
            b, rest = split2(rest)
            return jnp.concatenate([a, b, rest, jnp.zeros_like(a)], axis=0).astype(bf16)

        table = jnp.concatenate([three(bv_v[...]), three(bs_v[...])], axis=1)
        level_of = lax.broadcasted_iota(i32, (128, 128), 0)
        for i in range(7):
            chosen = (level_of % 32 == jnp.broadcast_to(lev_v[i:i + 1, :], (128, 128))) & (level_of < 96)
            bt_ref[i * 128:(i + 1) * 128, :] = dot(jnp.transpose(chosen.astype(f32)).astype(bf16), table)

    def places():
        for copy in list_copies:
            copy.wait()
        all_lists = lists[...]
        row_of = jnp.transpose(all_lists)
        numbers = all_lists.astype(f32)
        wide = jnp.concatenate([numbers[:, j // 2 * 32:j // 2 * 32 + 32] for j in range(8)], axis=1)
        number_hi, number_lo = (piece.astype(bf16) for piece in split2(wide))
        for i in range(7):
            at = slice(i * 128, (i + 1) * 128)
            channel = lax.broadcasted_iota(i32, (128, 256), 0) + i * 128
            match = channel == jnp.broadcast_to(row_of[0:1, :], (128, 256))
            for jlo in range(1, 4):
                match = match | (channel == jnp.broadcast_to(row_of[jlo * 32:jlo * 32 + 1, :], (128, 256)))
            hot = match.astype(f32).astype(bf16)
            hot_ref[at, :] = hot
            mask_ref[at, :] = (dot(hot, number_hi) + dot(hot, number_lo) == channel.astype(f32)).astype(f32)

    def split_coupling(k):
        coup_copy(k).wait()

        def some(i, _):
            at = pl.multiple_of(i * 32, 32)
            c = stage[k % 2, pl.ds(at, 32), :]
            hi = c.astype(bf16)
            to = pl.ds(pl.multiple_of(k * PART + i * 32, 32), 32)
            left_ref[to, 0:NCH] = hi
            left_ref[to, NCH:2 * NCH] = (c - hi.astype(f32)).astype(bf16)
            left_ref[to, 2 * NCH:3 * NCH] = hi
            return 0

        lax.fori_loop(0, PART // 32, some, 0)
        if k + 2 < NG // PART:
            coup_copy(k + 2).start()

    def add_fresh(n, rights):
        for d in range(1, 16):
            out(n, d).wait()
        hi, lo = split2(z_ref[n])
        picks = jnp.concatenate([a[:, jlo * 32:(jlo + 1) * 32] for jlo in range(4) for a in (hi, lo)], axis=1).astype(bf16)
        for i in range(NCH // STEP):
            at = pl.ds(i * STEP, STEP)
            four = dot(hot_ref[at, :], picks) * mask_ref[at, :]
            two = four[:, :128] + four[:, 128:]
            sums = dot(jnp.concatenate([two, two], axis=1).astype(bf16), fact_ref[n])
            for khi in range(2):
                value_at = bt_ref[at, khi * 128:(khi + 1) * 128]
                slope_at = bt_ref[at, 256 + khi * 128:256 + (khi + 1) * 128]
                for p in range(2):
                    col = khi * 512 + p * 128
                    fresh = value_at * sums[:, col + 256:col + 384] - slope_at * sums[:, col:col + 128]
                    cols = slice((khi * 2 + p) * 128, (khi * 2 + p + 1) * 128)
                    both = slice(n * 512 + (khi * 2 + p) * 128, n * 512 + (khi * 2 + p + 1) * 128)
                    total = prev_ref[at, both] + fresh
                    amp_ref[at, both] = total
                    high = total.astype(bf16)
                    rights[at, cols] = high
                    rights[pl.ds(NCH + i * STEP, STEP), cols] = high
                    rights[pl.ds(2 * NCH + i * STEP, STEP), cols] = (total - high.astype(f32)).astype(bf16)

    for n in range(2):
        for tail in (14, 15):
            ybuf[n, pl.ds(tail, 16, stride=16), :] = jnp.zeros((16, 128), f32)
    ring_begin(0)
    for n, k in ((0, 3), (1, 0), (1, 1), (1, 2), (1, 3)):
        core_copy(n, k).start()
    for copy in list_copies:
        copy.start()
    lists[here] = listed
    for k in range(2):
        coup_copy(k).start()
    for copy in prev_copies:
        copy.start()
    add_core(0, 3)
    phases()
    split_coupling(0)
    ring_pass(0)
    ring_begin(1)
    add_core(1, 3)
    tables()
    split_coupling(1)
    ring_end(0)
    split_coupling(2)
    ring_pass(1)
    places()
    for k in range(3, 8):
        split_coupling(k)
    for copy in prev_copies:
        copy.wait()
    add_fresh(0, right_first)
    ring_end(1)
    for m in range(2):
        first_ref[m * 1024:(m + 1) * 1024, :] = dot(left_ref[m * 1024:(m + 1) * 1024, :], right_first[...])
    add_fresh(1, right_ref)


def exchange(*operands):
    dma = pltpu.SemaphoreType.DMA
    block = pltpu.VMEM((2, 4, 16, 1792), f32)
    return pl.pallas_call(
        exchange_kernel,
        out_shape=(jax.ShapeDtypeStruct((NG, 3 * NCH), bf16), jax.ShapeDtypeStruct((3 * NCH, 512), bf16),
                   jax.ShapeDtypeStruct((NG, 512), f32), jax.ShapeDtypeStruct((NCH, 1024), f32)),
        in_specs=[HBM] * 11,
        out_specs=(VM,) * 4,
        scratch_shapes=[pltpu.VMEM((1792, 128), f32), pltpu.VMEM((4, 2, 32, 128), f32), pltpu.SMEM((56,), i32),
                        pltpu.SMEM((256,), f32), pltpu.SMEM((256,), f32), pltpu.VMEM((1, 256), f32),
                        pltpu.VMEM((32, 256), f32), pltpu.VMEM((32, 256), f32), pltpu.VMEM((7, 128), i32),
                        pltpu.VMEM((2, PART, NCH), f32), block, block, block,
                        pltpu.VMEM((2, 2, 16, HALF), f32), pltpu.VMEM((2, 2, 16, 1792), f32), pltpu.VMEM((2, 256, 128), f32),
                        pltpu.VMEM((16, 128), i32), pltpu.VMEM((256, 128), i32), pltpu.VMEM((2, 256, 128), f32),
                        pltpu.VMEM((NCH, 256), bf16), pltpu.VMEM((NCH, 256), f32), pltpu.VMEM((NCH, 512), f32),
                        pltpu.VMEM((2, 256, 1024), bf16),
                        pltpu.VMEM((NCH, 1024), f32), pltpu.VMEM((3 * NCH, 512), bf16),
                        dma((9,)), dma((8,)), dma((2,)), dma((2, 4)), dma((2, 4)), dma((2, 2)), dma((2, 2)),
                        dma((2, 2)), dma((2, 2)), dma((2, 2)), dma((2, 2)), dma((2, 16)), dma((2, 16)), dma((16,)), dma((16,))],
        compiler_params=pltpu.CompilerParams(vmem_limit_bytes=32 * 2**20, collective_id=0, has_side_effects=True),
        cost_estimate=pl.CostEstimate(flops=3 * NG * NCH * 1024, bytes_accessed=14 * 2**20, transcendentals=0),
        name="exchange",
    )(*(pltpu.with_memory_space_constraint(a, pltpu.HBM) for a in operands))


def spread_kernel(left_ref, right_ref, first_ref, amp_ref, amp_hbm, spec_hbm, obuf, asem, fsem, osem):
    bounds = (0, 1024, 1536, 1792, 2048)

    def amp_copy(s):
        return pltpu.make_async_copy(amp_ref.at[:, pl.ds(s * 128, 128)], amp_hbm.at[:, s, :], asem.at[s])

    def first_copy(s):
        return pltpu.make_async_copy(first_ref.at[:, pl.ds(s * 128, 128)], spec_hbm.at[:, s, :], fsem.at[s])

    def out_copy(m, s):
        at = pl.ds(bounds[m], bounds[m + 1] - bounds[m])
        return pltpu.make_async_copy(obuf.at[at, pl.ds(s * 128, 128)], spec_hbm.at[at, 4 + s, :], osem.at[m, s])

    for s in range(4):
        first_copy(s).start()
    for s in range(8):
        amp_copy(s).start()
    for m in range(4):
        at = pl.ds(bounds[m], bounds[m + 1] - bounds[m])
        obuf[at, :] = dot(left_ref[at, :], right_ref[...])
        for s in range(4):
            out_copy(m, s).start()
    for s in range(4):
        first_copy(s).wait()
    for s in range(8):
        amp_copy(s).wait()
    for m in range(4):
        for s in range(4):
            out_copy(m, s).wait()


def spread(*operands):
    dma = pltpu.SemaphoreType.DMA
    return pl.pallas_call(
        spread_kernel,
        out_shape=(jax.ShapeDtypeStruct((NCH, 8, 128), f32), jax.ShapeDtypeStruct((NG, 8, 128), f32)),
        in_specs=[VM] * 4,
        out_specs=(ANY, ANY),
        scratch_shapes=[pltpu.VMEM((NG, 512), f32), dma((8,)), dma((4,)), dma((4, 4))],
        compiler_params=pltpu.CompilerParams(vmem_limit_bytes=16 * 2**20),
        cost_estimate=pl.CostEstimate(flops=3 * NG * NCH * 1024, bytes_accessed=12 * 2**20, transcendentals=0),
        name="spread",
    )(*operands)


def shards(surface_rows, he_states, energies, state_phase, momentum_phase, bessel_value, bessel_slope,
           channel_l2, surface_list, previous, coupling):
    prev = previous.reshape(NCH, 2, 2, 2, 128).transpose(0, 1, 3, 2, 4).reshape(NCH, 8, 128)
    ready = exchange(surface_rows.reshape(1792, 128), he_states.reshape(4, 2, 32, 128), surface_list, energies, state_phase,
                     momentum_phase.reshape(1, 256), bessel_value, bessel_slope, channel_l2.reshape(7, 128), prev, coupling)
    amplitudes, spectrum = spread(*ready)

    def whole(a):
        return a.reshape(-1, 2, 2, 2, 128).transpose(0, 1, 3, 2, 4).reshape(-1, 2, 2, 256)

    return whole(amplitudes), whole(spectrum)


def solution(mesh):
    split = P(None, ("row", "ch"), None, None)
    return jax.shard_map(
        shards,
        mesh=mesh,
        in_specs=(P(None, None, "ch", "row"), P(None, "row"), P(), P(), P(), P(), P(), P(), P("ch"), split, P()),
        out_specs=(split, split),
        check_vma=False,
    )
```
